256 devices in a mesh: dp: 16 (over x, y_lo, core), pipe: 2 (over y_hi), tensor: 8 (over z).
Axes of the slice: x: 4, y: 4 (y_hi: 2, y_lo: 2; y = y_hi * 2 + y_lo), z: 8, core: 2. Of those that a mesh axis runs over, the one named last changes fastest.
Arguments:
- acts: bfloat16 [2, 2, 128, 8192], P('pipe', None, 'dp', 'tensor'), may hold values from -6 to 6
- output_gradient: bfloat16 [2, 128, 8192], P(None, 'dp', 'tensor'), may hold values from -6 to 6
- gate_up_weight: bfloat16 [2, 8192, 2, 14336], P('pipe', 'tensor', None, 'dp'), may hold values from -0.0625 to 0.0625
- down: bfloat16 [2, 14336, 8192], P('pipe', 'dp', 'tensor'), may hold values from -0.046875 to 0.046875
- adapter_first_weight: bfloat16 [2, 8192, 128], P('pipe', 'tensor'), may hold values from -0.0625 to 0.0625
- adapter_second_weight: bfloat16 [2, 2, 64, 14336], P('pipe', None, None, 'dp'), may hold values from -0.29882812 to 0.29882812
Outputs:
- grad_inputs: bfloat16 [2, 2, 128, 8192], P('pipe', None, 'dp', 'tensor')
- grad_lora_down: float32 [2, 8192, 128], P('pipe', 'tensor')
- grad_lora_up: float32 [2, 2, 64, 14336], P('pipe', None, None, 'dp')
The draws below stay inside these ranges and needn't reach their ends.
All inputs are finite; a program needn't handle non-finite values.
Results may differ from the reference program's by a relative error of at most 0.014.
Values may be sent and summed in bfloat16 or wider, within the bound.
No kernel may reach another device: no remote copies, remote signals or barrier semaphores. Data moves between devices by JAX's collectives and lax.ppermute only.
A program may use at most 64 MiB of HBM per device.

```python
import math
import jax
import jax.numpy as jnp
from jax import lax

MODEL_WIDTH = 8192
HIDDEN_UNITS = 14336
ADAPTER_RANK = 64
MICRO_BATCHES = 2
LAYER_COUNT = 2
MICRO_TOKENS = 128
N_TENSOR = 8


def steps_of(stream_key, dims, pieces, smallest, high):
    def one(position, blocks):
        heights = jax.random.uniform(jax.random.fold_in(jax.random.fold_in(stream_key, 6), position), (blocks,), jnp.float32, smallest / len(pieces), high / len(pieces))
        return jnp.repeat(jnp.exp(heights), dims[position] // blocks).reshape((-1,) + (1,) * (len(dims) - position - 1))

    factor_of = one(*pieces[0])
    for cut in pieces[1:]:
        factor_of = factor_of * one(*cut)
    return factor_of


def normal_values(key, dims, width, most, cuts=(), dtype=jnp.bfloat16):
    gain = steps_of(key, dims, cuts, -0.22, 0.18) if cuts else 1.0
    drawn = jax.random.normal(key, dims, jnp.float32) * width * gain
    return jnp.minimum(jnp.maximum(drawn, -most), most).astype(dtype)


def setup_inputs(seed: int = 0) -> dict:
    seeds = jax.random.split(jax.random.key(seed), 7)
    return {
        "acts": normal_values(seeds[0], (LAYER_COUNT, MICRO_BATCHES, MICRO_TOKENS, MODEL_WIDTH), 1.0, 6.0, ((0, 2), (2, 16), (3, 8))),
        "output_gradient": normal_values(seeds[1], (MICRO_BATCHES, MICRO_TOKENS, MODEL_WIDTH), 1.0, 6.0, ((1, 16), (2, 8))),
        "gate_up_weight": normal_values(seeds[2], (LAYER_COUNT, MODEL_WIDTH, 2, HIDDEN_UNITS), MODEL_WIDTH ** -0.5, 0.0625, ((0, 2), (1, 8), (3, 16))),
        "down": normal_values(seeds[3], (LAYER_COUNT, HIDDEN_UNITS, MODEL_WIDTH), HIDDEN_UNITS ** -0.5, 0.046875, ((0, 2), (1, 16), (2, 8))),
        "adapter_first_weight": normal_values(seeds[4], (LAYER_COUNT, MODEL_WIDTH, 2 * ADAPTER_RANK), MODEL_WIDTH ** -0.5, 0.0625, ((0, 2), (1, 8))),
        "adapter_second_weight": normal_values(seeds[5], (LAYER_COUNT, 2, ADAPTER_RANK, HIDDEN_UNITS), 0.05, 0.29882812, ((0, 2), (3, 16))),
    }


adapter_scale = 2.0

def blockwise(left_mat, right_mat, right_axis):
    block_cols = MODEL_WIDTH // N_TENSOR
    summed = None
    for block_num in range(N_TENSOR):
        start_col = block_num * block_cols
        left_part = left_mat[:, start_col:start_col + block_cols]
        if right_axis == 0:
            right_part = right_mat[start_col:start_col + block_cols]
            dim_spec = (((1,), (0,)), ((), ()))
        else:
            right_part = right_mat[:, start_col:start_col + block_cols]
            dim_spec = (((1,), (1,)), ((), ()))
        partial_sum = lax.dot_general(left_part, right_part, dim_spec, preferred_element_type=jnp.float32)
        summed = partial_sum if block_num == 0 else summed + partial_sum
    return summed

def layer_backward(inputs_x, upstream, joined_weight, down_weight, adapter_first, adapter_second):
    token_count = inputs_x.shape[0]
    joined_flat = joined_weight.reshape(MODEL_WIDTH, 2 * HIDDEN_UNITS)
    second_float_copy = adapter_second.astype(jnp.float32)
    low_bf = blockwise(inputs_x, adapter_first, 0).astype(jnp.bfloat16)
    reduced_triple = low_bf.astype(jnp.float32).reshape(token_count, 2, ADAPTER_RANK)
    frozen_preact = blockwise(inputs_x, joined_flat, 0).reshape(token_count, 2, HIDDEN_UNITS)
    preactivation = frozen_preact + adapter_scale * jnp.einsum('bnd,ndc->bnc', reduced_triple, second_float_copy)
    hidden_grad = blockwise(upstream, down_weight, 1)
    gate_pre = preactivation[:, 0]
    up_pre = preactivation[:, 1]
    gate_sig = jax.nn.sigmoid(gate_pre)
    gate_grad = hidden_grad * up_pre * gate_sig * (1.0 + gate_pre * (1.0 - gate_sig))
    up_grad = hidden_grad * gate_pre * gate_sig
    act_grad = jnp.stack((gate_grad, up_grad), axis=1).astype(jnp.bfloat16)
    act_float = act_grad.astype(jnp.float32)
    backward_brain = jnp.einsum('tkf,krf->tkr', act_float, second_float_copy).reshape(token_count, 2 * ADAPTER_RANK).astype(jnp.bfloat16)
    gradient_input = lax.dot_general(act_grad.reshape(token_count, 2 * HIDDEN_UNITS), joined_flat, (((1,), (1,)), ((), ())), preferred_element_type=jnp.float32)
    gradient_input = gradient_input + adapter_scale * lax.dot_general(backward_brain, adapter_first, (((1,), (1,)), ((), ())), preferred_element_type=jnp.float32)
    first_factor_term = lax.dot_general(inputs_x, backward_brain, (((0,), (0,)), ((), ())), preferred_element_type=jnp.float32)
    second_factor_term = jnp.einsum('tkr,tkf->krf', reduced_triple, act_float)
    return (gradient_input.astype(jnp.bfloat16), first_factor_term, second_factor_term)

def reference(acts, output_gradient, gate_up_weight, down, adapter_first_weight, adapter_second_weight):
    factor_value = adapter_scale / math.sqrt(MICRO_BATCHES * MICRO_TOKENS)
    upstream_gradients = [output_gradient[microbatch_position] for microbatch_position in range(MICRO_BATCHES)]
    grad_layers = []
    down_layers = []
    up_layers = []
    for layer_position in range(LAYER_COUNT - 1, -1, -1):
        outputs_list = []
        down_total = jnp.zeros((MODEL_WIDTH, 2 * ADAPTER_RANK), jnp.float32)
        up_total = jnp.zeros((2, ADAPTER_RANK, HIDDEN_UNITS), jnp.float32)
        for microbatch_position in range(MICRO_BATCHES):
            gradient_input, first_factor_term, second_factor_term = layer_backward(acts[layer_position, microbatch_position], upstream_gradients[microbatch_position], gate_up_weight[layer_position], down[layer_position], adapter_first_weight[layer_position], adapter_second_weight[layer_position])
            outputs_list.append(gradient_input)
            down_total = down_total + first_factor_term
            up_total = up_total + second_factor_term
        upstream_gradients = outputs_list
        grad_layers.insert(0, jnp.stack(outputs_list))
        down_layers.insert(0, down_total * factor_value)
        up_layers.insert(0, up_total * factor_value)
    return (jnp.stack(grad_layers), jnp.stack(down_layers), jnp.stack(up_layers))
```

```python
import math

import jax
import jax.numpy as jnp
from jax import lax
from jax.sharding import Mesh, PartitionSpec as P

adapter_scale = 2.0
CHIPS = ("x", "yl")
F32 = jnp.float32
BF16 = jnp.bfloat16


def dot_nn(a, b):
    return jnp.dot(a, b, preferred_element_type=F32)


def dot_nt(a, b):
    return lax.dot_general(a, b, (((1,), (1,)), ((), ())), preferred_element_type=F32)


def dot_tn(a, b):
    return lax.dot_general(a, b, (((0,), (0,)), ((), ())), preferred_element_type=F32)


def core_swap(block):
    return lax.ppermute(block, "core", [(0, 1), (1, 0)])


def to_all_chips(block, axis):
    n = lax.axis_size(axis)
    return lax.all_to_all(jnp.broadcast_to(block[None], (n,) + block.shape), axis, 0, 0)


def gather_dp(block):
    mine = to_all_chips(block, CHIPS)
    mine = mine.reshape((-1,) + block.shape[1:])
    return jnp.concatenate([mine, core_swap(mine)], axis=0)


def scatter_z(partial):
    n = lax.axis_size("z")
    parts = partial.astype(BF16).reshape(n, -1, partial.shape[1])
    return jnp.sum(lax.all_to_all(parts, "z", 0, 0).astype(F32), axis=0)


def swiglu_back(pre, hidden):
    half = pre.shape[1] // 2
    gate, up = pre[:, :half].astype(F32), pre[:, half:].astype(F32)
    sig = 1.0 / (1.0 + jnp.exp(-gate))
    gate_grad = hidden * up * sig * (1.0 + gate * (1.0 - sig))
    up_grad = hidden * gate * sig
    return jnp.concatenate([gate_grad, up_grad], axis=1).astype(BF16)


def local(acts, output_gradient, gate_up_weight, down, adapter_first_weight, adapter_second_weight):
    upper = lax.axis_index("pipe") == 1
    micro, rows, feat = acts.shape[1:]
    hidden_units = down.shape[1]
    rank = adapter_second_weight.shape[2]
    own = micro * rows
    weight = gate_up_weight[0].reshape(feat, 2 * hidden_units)
    down_weight = down[0]
    first = adapter_first_weight[0]
    second = adapter_second_weight[0]
    tokens = own * lax.axis_size(("x", "yl", "core"))
    half = tokens // 2
    factor = adapter_scale / math.sqrt(tokens)

    def adapter_up(low):
        low = low.astype(BF16)
        return jnp.concatenate(
            [dot_nn(low[:, :rank], second[0]), dot_nn(low[:, rank:], second[1])], axis=1
        )

    def adapter_back(act):
        return jnp.concatenate(
            [dot_nt(act[:, :hidden_units], second[0]), dot_nt(act[:, hidden_units:], second[1])], axis=1
        )

    def input_partial(act):
        back = adapter_back(act)
        return dot_nt(act, weight) + adapter_scale * dot_nt(back.astype(BF16), first), back

    def core_sum(partial):
        partial = partial.astype(BF16)
        return partial[:half].astype(F32) + core_swap(partial[half:]).astype(F32)

    both = jnp.concatenate([acts[0].reshape(own, feat), output_gradient.reshape(own, feat)], axis=1)
    both = gather_dp(both)
    inputs, upstream = both[:, :feat], both[:, feat:]

    low_part = dot_nn(inputs, first)
    pre_part = dot_nn(inputs, weight) + adapter_scale * adapter_up(low_part)
    hidden_part = dot_nt(upstream, down_weight)
    summed = scatter_z(jnp.concatenate([pre_part, low_part, hidden_part], axis=1))
    width = 2 * hidden_units
    pre_own = summed[:, :width]
    act_own = swiglu_back(pre_own, summed[:, width + 2 * rank:])
    sent = jnp.concatenate(
        [jnp.where(upper, act_own, pre_own.astype(BF16)), summed[:, width:width + 2 * rank].astype(BF16)],
        axis=1,
    )
    held = lax.all_gather(sent, "z", axis=0, tiled=True)
    act_or_pre, low = held[:, :width], held[:, width:]
    part, back = input_partial(act_or_pre)
    mine = core_sum(jnp.concatenate([part, back], axis=1))
    mine = lax.all_to_all(mine.astype(BF16).reshape(-1, own, mine.shape[1]), CHIPS, 0, 0)
    mine = jnp.sum(mine.astype(F32), axis=0).astype(BF16)
    grad_one, back_one = mine[:, :feat], mine[:, feat:]

    handed = lax.ppermute(grad_one, "pipe", [(1, 0)])
    sent = jnp.where(upper, jnp.pad(back_one, ((0, 0), (0, feat - 2 * rank))), handed)
    upstream = gather_dp(sent)
    back_upper = upstream[:, :2 * rank]
    hidden_own = scatter_z(dot_nt(upstream, down_weight))
    hidden_all = to_all_chips(hidden_own.astype(BF16), "z").reshape(tokens, hidden_units)
    act_lower = swiglu_back(act_or_pre, hidden_all.astype(F32))
    part, back = input_partial(act_lower)
    mine = core_sum(part).astype(BF16).reshape(-1, own, feat)
    back = core_sum(back).astype(BF16)
    chips = mine.shape[0]
    back = jnp.broadcast_to(back.reshape(1, -1, feat), (chips, back.size // feat, feat))
    got = lax.all_to_all(jnp.concatenate([mine, back], axis=1), CHIPS, 0, 0)
    got = jnp.sum(got.astype(F32), axis=0).astype(BF16)
    grad_zero = got[:own]
    back_half = got[own:].reshape(half, 2 * rank)
    back_lower = jnp.concatenate([back_half, core_swap(back_half)], axis=0)

    act = jnp.where(upper, act_or_pre, act_lower)
    grad_up = jnp.stack(
        [
            dot_tn(low[:, :rank], act[:, :hidden_units]),
            dot_tn(low[:, rank:], act[:, hidden_units:]),
        ]
    )
    grad_down = dot_tn(inputs, jnp.where(upper, back_upper, back_lower))
    grad_inputs = jnp.where(upper, grad_one, grad_zero).reshape(1, micro, rows, feat)
    return grad_inputs, (grad_down * factor)[None], (grad_up * factor)[None]


def solution(mesh):
    sizes = dict(mesh.shape)
    fine = Mesh(
        mesh.devices.reshape(sizes["dp"] // 4, 2, 2, sizes["pipe"], sizes["tensor"]),
        ("x", "yl", "core", "pipe", "z"),
    )
    dp = ("x", "yl", "core")
    in_specs = (
        P("pipe", None, dp, "z"),
        P(None, dp, "z"),
        P("pipe", "z", None, dp),
        P("pipe", dp, "z"),
        P("pipe", "z", None),
        P("pipe", None, None, dp),
    )
    out_specs = (
        P("pipe", None, dp, "z"),
        P("pipe", "z", None),
        P("pipe", None, None, dp),
    )
    return jax.shard_map(local, mesh=fine, in_specs=in_specs, out_specs=out_specs, check_vma=False)
```

```python
import math

import jax
import jax.numpy as jnp
from jax import lax
from jax.sharding import Mesh, PartitionSpec as P

adapter_scale = 2.0
CHIPS = ("x", "yl")
F32 = jnp.float32
BF16 = jnp.bfloat16


def dot_nn(a, b):
    return jnp.dot(a, b, preferred_element_type=F32)


def dot_nt(a, b):
    return lax.dot_general(a, b, (((1,), (1,)), ((), ())), preferred_element_type=F32)


def dot_tn(a, b):
    return lax.dot_general(a, b, (((0,), (0,)), ((), ())), preferred_element_type=F32)


def core_swap(block):
    return lax.ppermute(block, "core", [(0, 1), (1, 0)])


def to_all_chips(block, axis):
    n = lax.axis_size(axis)
    return lax.all_to_all(jnp.broadcast_to(block[None], (n,) + block.shape), axis, 0, 0)


def gather_dp(block):
    mine = to_all_chips(block, CHIPS)
    mine = mine.reshape((-1,) + block.shape[1:])
    return jnp.concatenate([mine, core_swap(mine)], axis=0)


def scatter_z(partial):
    n = lax.axis_size("z")
    parts = partial.astype(BF16).reshape(n, -1, partial.shape[1])
    return jnp.sum(lax.all_to_all(parts, "z", 0, 0).astype(F32), axis=0)


def ring(step):
    n = lax.axis_size("z")
    return [(i, (i + step) % n) for i in range(n)]


def ring_scatter_z(partial):
    n = lax.axis_size("z")
    me = lax.axis_index("z")
    parts = partial.reshape(n, -1, partial.shape[1])

    def part(step):
        return lax.dynamic_index_in_dim(parts, lax.rem(me + step + n, n), 0, keepdims=False)

    def plus(total, step):
        return total.astype(F32) + part(step).astype(F32)

    ahead, behind = n // 2, n - 1 - n // 2
    up, back = part(ahead), part(-behind)
    for step in range(ahead - 1, -1, -1):
        up = lax.ppermute(up, "z", ring(1))
        if step < behind:
            back = lax.ppermute(back, "z", ring(-1))
        if step:
            up = plus(up, step).astype(BF16)
            if step < behind:
                back = plus(back, -step).astype(BF16)
    return plus(up, 0) + back.astype(F32)


def ring_gather_z(block):
    n = lax.axis_size("z")
    me = lax.axis_index("z")
    rows = block.shape[0]
    out = jnp.zeros((n * rows, block.shape[1]), block.dtype)

    def put(out, piece, step):
        return lax.dynamic_update_slice(out, piece, (lax.rem(me + step + n, n) * rows, 0))

    out = put(out, block, 0)
    up = back = block
    for step in range(1, n // 2 + 1):
        back = lax.ppermute(back, "z", ring(-1))
        if step < n // 2:
            up = lax.ppermute(up, "z", ring(1))
            out = put(out, up, -step)
        out = put(out, back, step)
    return out


def swiglu_back(pre, hidden):
    half = pre.shape[1] // 2
    gate, up = pre[:, :half].astype(F32), pre[:, half:].astype(F32)
    sig = 1.0 / (1.0 + jnp.exp(-gate))
    gate_grad = hidden * up * sig * (1.0 + gate * (1.0 - sig))
    up_grad = hidden * gate * sig
    return jnp.concatenate([gate_grad, up_grad], axis=1).astype(BF16)


def local(acts, output_gradient, gate_up_weight, down, adapter_first_weight, adapter_second_weight):
    upper = lax.axis_index("pipe") == 1
    micro, rows, feat = acts.shape[1:]
    hidden_units = down.shape[1]
    rank = adapter_second_weight.shape[2]
    own = micro * rows
    weight = gate_up_weight[0].reshape(feat, 2 * hidden_units)
    down_weight = down[0]
    first = adapter_first_weight[0]
    second = adapter_second_weight[0]
    tokens = own * lax.axis_size(("x", "yl", "core"))
    half = tokens // 2
    factor = adapter_scale / math.sqrt(tokens)

    def adapter_up(low):
        low = low.astype(BF16)
        return jnp.concatenate(
            [dot_nn(low[:, :rank], second[0]), dot_nn(low[:, rank:], second[1])], axis=1
        )

    def adapter_back(act):
        return jnp.concatenate(
            [dot_nt(act[:, :hidden_units], second[0]), dot_nt(act[:, hidden_units:], second[1])], axis=1
        )

    def input_partial(act):
        back = adapter_back(act)
        return dot_nt(act, weight) + adapter_scale * dot_nt(back.astype(BF16), first), back

    def core_sum(partial):
        partial = partial.astype(BF16)
        return partial[:half].astype(F32) + core_swap(partial[half:]).astype(F32)

    both = jnp.concatenate([acts[0].reshape(own, feat), output_gradient.reshape(own, feat)], axis=1)
    both = gather_dp(both)
    inputs, upstream = both[:, :feat], both[:, feat:]

    low_part = dot_nn(inputs, first)
    pre_part = dot_nn(inputs, weight) + adapter_scale * adapter_up(low_part)
    hidden_part = dot_nt(upstream, down_weight)
    summed = ring_scatter_z(jnp.concatenate([pre_part, low_part, hidden_part], axis=1).astype(BF16))
    width = 2 * hidden_units
    pre_own = summed[:, :width]
    act_own = swiglu_back(pre_own, summed[:, width + 2 * rank:])
    sent = jnp.concatenate(
        [jnp.where(upper, act_own, pre_own.astype(BF16)), summed[:, width:width + 2 * rank].astype(BF16)],
        axis=1,
    )
    held = ring_gather_z(sent)
    act_or_pre, low = held[:, :width], held[:, width:]
    part, back = input_partial(act_or_pre)
    mine = core_sum(jnp.concatenate([part, back], axis=1))
    mine = mine.astype(BF16).reshape(-1, 1, own, mine.shape[1])
    chips, wide = mine.shape[0], mine.shape[3]
    mine = jnp.broadcast_to(mine, (chips, 2, own, wide)).reshape(2 * chips, own, wide)
    mine = lax.all_to_all(mine, CHIPS + ("pipe",), 0, 0).reshape(chips, 2, own, wide)
    mine = jnp.sum(mine[:, 1].astype(F32), axis=0).astype(BF16)
    grad_one, back_one = mine[:, :feat], mine[:, feat:]

    sent = jnp.where(upper, jnp.pad(back_one, ((0, 0), (0, feat - 2 * rank))), grad_one)
    upstream = gather_dp(sent)
    back_upper = upstream[:, :2 * rank]
    hidden_own = scatter_z(dot_nt(upstream, down_weight))
    hidden_all = ring_gather_z(hidden_own.astype(BF16))
    act_lower = swiglu_back(act_or_pre, hidden_all.astype(F32))
    part, back = input_partial(act_lower)
    mine = core_sum(part).astype(BF16).reshape(-1, own, feat)
    back = core_sum(back).astype(BF16)
    back = jnp.broadcast_to(back.reshape(1, -1, feat), (chips, back.size // feat, feat))
    got = lax.all_to_all(jnp.concatenate([mine, back], axis=1), CHIPS, 0, 0)
    got = jnp.sum(got.astype(F32), axis=0).astype(BF16)
    grad_zero = got[:own]
    back_half = got[own:].reshape(half, 2 * rank)
    back_lower = jnp.concatenate([back_half, core_swap(back_half)], axis=0)

    act = jnp.where(upper, act_or_pre, act_lower)
    grad_up = jnp.stack(
        [
            dot_tn(low[:, :rank], act[:, :hidden_units]),
            dot_tn(low[:, rank:], act[:, hidden_units:]),
        ]
    )
    grad_down = dot_tn(inputs, jnp.where(upper, back_upper, back_lower))
    grad_inputs = jnp.where(upper, grad_one, grad_zero).reshape(1, micro, rows, feat)
    return grad_inputs, (grad_down * factor)[None], (grad_up * factor)[None]


def solution(mesh):
    sizes = dict(mesh.shape)
    fine = Mesh(
        mesh.devices.reshape(sizes["dp"] // 4, 2, 2, sizes["pipe"], sizes["tensor"]),
        ("x", "yl", "core", "pipe", "z"),
    )
    dp = ("x", "yl", "core")
    in_specs = (
        P("pipe", None, dp, "z"),
        P(None, dp, "z"),
        P("pipe", "z", None, dp),
        P("pipe", dp, "z"),
        P("pipe", "z", None),
        P("pipe", None, None, dp),
    )
    out_specs = (
        P("pipe", None, dp, "z"),
        P("pipe", "z", None),
        P("pipe", None, None, dp),
    )
    return jax.shard_map(local, mesh=fine, in_specs=in_specs, out_specs=out_specs, check_vma=False)
```

```python
import functools
import math

import jax
import jax.numpy as jnp
from jax import lax
from jax.experimental import pallas as pl
from jax.experimental.pallas import tpu as pltpu
from jax.sharding import Mesh, PartitionSpec as P

adapter_scale = 2.0
CHIPS = ("x", "yl")
F32 = jnp.float32
BF16 = jnp.bfloat16
VMEM_LIMIT = 40 * 2**20


def dot_nn(a, b):
    return jnp.dot(a, b, preferred_element_type=F32)


def dot_nt(a, b):
    return lax.dot_general(a, b, (((1,), (1,)), ((), ())), preferred_element_type=F32)


def dot_tn(a, b):
    return lax.dot_general(a, b, (((0,), (0,)), ((), ())), preferred_element_type=F32)


def kept(shape, dtype=BF16):
    return pltpu.VMEM(shape, dtype)


def call(kernel, outs, place, *args, scratch=(), flops=0):
    size = sum(a.size * a.dtype.itemsize for a in args)
    return pl.pallas_call(
        kernel,
        out_shape=outs,
        in_specs=[pl.BlockSpec(memory_space=pltpu.SMEM)]
        + [pl.BlockSpec(memory_space=pltpu.VMEM)] * len(args),
        out_specs=jax.tree.map(lambda _: pl.BlockSpec(memory_space=pltpu.VMEM), outs),
        scratch_shapes=list(scratch),
        compiler_params=pltpu.CompilerParams(vmem_limit_bytes=VMEM_LIMIT),
        cost_estimate=pl.CostEstimate(flops=flops, bytes_accessed=size, transcendentals=0),
    )(place, *[pltpu.with_memory_space_constraint(a, pltpu.VMEM) for a in args])


def core_swap(block):
    return lax.ppermute(block, "core", [(0, 1), (1, 0)])


def ring(block, step):
    n = lax.axis_size("z")
    return lax.ppermute(block, "z", [(i, (i + step) % n) for i in range(n)])


def swiglu_back(gate, up, hidden):
    sig = 1.0 / (1.0 + jnp.exp(-gate))
    gate_grad = hidden * up * sig * (1.0 + gate * (1.0 - sig))
    up_grad = hidden * gate * sig
    return gate_grad.astype(BF16), up_grad.astype(BF16)


def tiles(width, most=512):
    return [(lo, min(most, width - lo)) for lo in range(0, width, most)]


def forward_kernel(place, mine, other, weight, down, first, second, up, back, parts):
    n, rows, width = parts.shape
    feat = first.shape[0]
    hidden, rank = second.shape[2], second.shape[1]
    x = jnp.concatenate([mine[:, :feat], other[:, :feat]], axis=0)
    low = dot_nn(x, first[...]).astype(BF16)
    parts[:, :, 2 * hidden:2 * hidden + 2 * rank] = low.reshape(n, rows, 2 * rank)
    for k in range(2):
        for lo, size in tiles(hidden):
            at = k * hidden + lo
            pre = dot_nn(x, weight[:, at:at + size])
            pre += adapter_scale * dot_nn(low[:, k * rank:(k + 1) * rank], second[k, :, lo:lo + size])
            parts[:, :, at:at + size] = pre.astype(BF16).reshape(n, rows, size)
    g = jnp.concatenate([mine[:, feat:], other[:, feat:]], axis=0)
    at = 2 * hidden + 2 * rank
    for lo, size in tiles(hidden):
        part = dot_nt(g, down[lo:lo + size, :])
        parts[:, :, at + lo:at + lo + size] = part.astype(BF16).reshape(n, rows, size)
    far = lax.rem(place[0] + n // 2, n)
    up[...] = parts[far, :, :width // 2]
    back[...] = parts[far, :, width // 2:]


def ring_add_kernel(step, place, up_in, back_in, parts, up, back):
    n, _, width = parts.shape
    half = width // 2
    ahead = lax.rem(place[0] + step, n)
    behind = lax.rem(place[0] + n - step, n)
    if up_in.shape[1] == half:
        up[:, :half] = (up_in[...].astype(F32) + parts[ahead, :, :half].astype(F32)).astype(BF16)
        up[:, half:] = parts[ahead, :, half:]
        back[:, :half] = parts[behind, :, :half]
        back[:, half:] = (back_in[...].astype(F32) + parts[behind, :, half:].astype(F32)).astype(BF16)
    else:
        up[...] = (up_in[...].astype(F32) + parts[ahead].astype(F32)).astype(BF16)
        back[...] = (back_in[...].astype(F32) + parts[behind].astype(F32)).astype(BF16)


def middle_kernel(place, up_in, back_in, parts, sent):
    total = up_in[...].astype(F32) + back_in[...].astype(F32) + parts[place[0]].astype(F32)
    width = sent.shape[1]
    hidden = total.shape[1] - width
    gate, up = total[:, :hidden], total[:, hidden:2 * hidden]
    gate_grad, up_grad = swiglu_back(gate, up, total[:, width:])
    upper = place[1] == 1
    sent[:, :hidden] = jnp.where(upper, gate_grad, gate.astype(BF16))
    sent[:, hidden:2 * hidden] = jnp.where(upper, up_grad, up.astype(BF16))
    sent[:, 2 * hidden:] = total[:, 2 * hidden:width].astype(BF16)


def collect(place, pieces, whole):
    n, rows = len(pieces), pieces[0].shape[0]
    for step, piece in enumerate(pieces):
        at = pl.multiple_of(lax.rem(place[0] + step, n) * rows, rows)
        whole[pl.ds(at, rows), :] = piece[...]


def input_partials(act, weight, first, second, mine, other):
    feat = first.shape[0]
    hidden, rank = second.shape[2], second.shape[1]
    half = mine.shape[0]
    back = jnp.concatenate(
        [dot_nt(act[:, k * hidden:(k + 1) * hidden], second[k]) for k in range(2)], axis=1
    )
    mine[:, feat:] = back[:half]
    other[:, feat:] = back[half:].astype(BF16)
    scaled = (adapter_scale * back).astype(BF16)
    for lo, size in tiles(feat, 256):
        part = dot_nt(act[:, :2 * hidden], weight[lo:lo + size, :]) + dot_nt(scaled, first[lo:lo + size, :])
        mine[:, lo:lo + size] = part[:half]
        other[:, lo:lo + size] = part[half:].astype(BF16)


def backward_kernel(count, place, *refs):
    pieces = refs[:count]
    weight, first, second, whole, mine, other = refs[count:]
    collect(place, pieces, whole)
    input_partials(whole, weight, first, second, mine, other)


def lower_kernel(count, place, *refs):
    pieces = refs[:count]
    whole, weight, first, second, act, mine, other, hidden_grad = refs[count:]
    collect(place, pieces, hidden_grad)
    hidden = hidden_grad.shape[1]
    for lo, size in tiles(hidden, 128):
        gate_grad, up_grad = swiglu_back(
            whole[:, lo:lo + size].astype(F32),
            whole[:, hidden + lo:hidden + lo + size].astype(F32),
            hidden_grad[:, lo:lo + size].astype(F32),
        )
        act[:, lo:lo + size] = gate_grad
        act[:, hidden + lo:hidden + lo + size] = up_grad
    input_partials(act, weight, first, second, mine, other)


def to_both_kernel(place, mine, other, out):
    total = (mine[...] + other[...].astype(F32)).astype(BF16)
    chips, sections, rows, width = out.shape
    for section in range(sections):
        out[:, section] = total.reshape(chips, rows, width)


def hand_kernel(place, got, grad, out):
    feat = grad.shape[1]
    total = jnp.sum(got[:, 1].astype(F32), axis=0).astype(BF16)
    grad[...] = total[:, :feat]
    back = jnp.concatenate([total[:, feat:], jnp.zeros((total.shape[0], 2 * feat - total.shape[1]), BF16)], axis=1)
    message = jnp.where(place[1] == 1, back, total[:, :feat])
    for chip in range(out.shape[0]):
        out[chip] = message


def last_message_kernel(place, mine, other, out):
    total = (mine[...] + other[...].astype(F32)).astype(BF16)
    chips, rows, _ = out.shape
    wide = total.shape[1] - (out.shape[2] - total.shape[1]) // (chips - 1)
    rank = total.shape[1] - wide
    out[:, :, :wide] = total[:, :wide].reshape(chips, rows, wide)
    for chip in range(chips):
        block = total[chip * rows:(chip + 1) * rows, wide:]
        for target in range(chips):
            out[target, :, wide + chip * rank:wide + (chip + 1) * rank] = block


def last_sum_kernel(place, got, grad_one, grad, back):
    chips, rows, _ = got.shape
    feat, rank = grad.shape[1], back.shape[1]
    total = jnp.sum(got[...].astype(F32), axis=0).astype(BF16)
    grad[...] = jnp.where(place[1] == 1, grad_one[...], total[:, :feat])
    for chip in range(chips):
        back[chip * rows:(chip + 1) * rows, :] = total[:, feat + chip * rank:feat + (chip + 1) * rank]


def grad_up_kernel(factor, place, whole, act, out):
    hidden, rank = out.shape[2], out.shape[1]
    for k in range(2):
        low = whole[:, 2 * hidden + k * rank:2 * hidden + (k + 1) * rank]
        for lo, size in tiles(hidden):
            at = k * hidden + lo
            used = jnp.where(place[1] == 1, whole[:, at:at + size], act[:, at:at + size])
            out[k, :, lo:lo + size] = dot_tn(low, used) * factor


def grad_down_kernel(factor, place, mine, other, upper_mine, upper_other, lower_mine, lower_other, out):
    feat, rank = out.shape
    upper = place[1] == 1
    back = jnp.where(upper, upper_mine[:, :rank], lower_mine[...])
    back_other = jnp.where(upper, upper_other[:, :rank], lower_other[...])
    for lo, size in tiles(feat, 256):
        part = dot_tn(mine[:, lo:lo + size], back) + dot_tn(other[:, lo:lo + size], back_other)
        out[lo:lo + size, :] = part * factor


def local(acts, output_gradient, gate_up_weight, down, adapter_first_weight, adapter_second_weight):
    micro, rows, feat = acts.shape[1:]
    hidden = down.shape[1]
    rank = adapter_second_weight.shape[2]
    own = micro * rows
    weight = gate_up_weight[0].reshape(feat, 2 * hidden)
    down_weight = down[0]
    first = adapter_first_weight[0]
    second = adapter_second_weight[0]
    chips = lax.axis_size(CHIPS)
    tokens = own * chips * lax.axis_size("core")
    half = tokens // 2
    n = lax.axis_size("z")
    block = tokens // n
    width = 2 * hidden + 2 * rank
    factor = adapter_scale / math.sqrt(tokens)
    place = jnp.stack([lax.axis_index("z"), lax.axis_index("pipe")]).astype(jnp.int32)

    def ring_gather(piece):
        up = back = piece
        ups, backs = [], []
        for step in range(1, n // 2 + 1):
            back = ring(back, -1)
            backs.append(back)
            if step < n // 2:
                up = ring(up, 1)
                ups.append(up)
        return [piece] + backs + ups[::-1]

    def to_all_chips(message):
        got = lax.all_to_all(message, CHIPS, 0, 0)
        got = got.reshape(half, message.shape[2])
        return got, core_swap(got)

    both = jnp.concatenate([acts[0].reshape(own, feat), output_gradient.reshape(own, feat)], axis=1)
    mine, other = to_all_chips(jnp.broadcast_to(both[None], (chips, own, 2 * feat)))

    full = width + hidden
    up, back, parts = call(
        forward_kernel,
        (kept((block, full // 2)), kept((block, full // 2)), kept((n, block, full))),
        place, mine, other, weight, down_weight, first, second,
        flops=2 * tokens * feat * full,
    )
    for step in range(n // 2 - 1, -1, -1):
        up, back = ring(up, 1), ring(back, -1)
        if step:
            up, back = call(
                functools.partial(ring_add_kernel, step),
                (kept((block, full)), kept((block, full))), place, up, back, parts,
            )
    sent = call(middle_kernel, kept((block, width)), place, up, back, parts)
    whole, half_mine, half_other = call(
        functools.partial(backward_kernel, n),
        (kept((tokens, width)), kept((half, feat + 2 * rank), F32), kept((half, feat + 2 * rank))),
        place, *ring_gather(sent), weight, first, second,
        flops=2 * tokens * feat * width,
    )
    message = call(
        to_both_kernel, kept((chips, 2, own, feat + 2 * rank)), place, half_mine, core_swap(half_other)
    )
    got = lax.all_to_all(message.reshape(chips * 2, own, -1), CHIPS + ("pipe",), 0, 0)
    grad_one, message = call(
        hand_kernel, (kept((own, feat)), kept((chips, own, feat))), place, got.reshape(message.shape)
    )

    next_mine, next_other = to_all_chips(message)
    upstream = jnp.concatenate([next_mine, next_other], axis=0)
    hidden_part = dot_nt(upstream, down_weight).astype(BF16).reshape(n, block, hidden)
    hidden_own = lax.all_to_all(hidden_part, "z", 0, 0)
    hidden_own = jnp.sum(hidden_own.astype(F32), axis=0).astype(BF16)
    act, half_mine, half_other = call(
        functools.partial(lower_kernel, n),
        (kept((tokens, 2 * hidden)), kept((half, feat + 2 * rank), F32), kept((half, feat + 2 * rank))),
        place, *ring_gather(hidden_own), whole, weight, first, second,
        scratch=[pltpu.VMEM((tokens, hidden), BF16)],
        flops=2 * tokens * feat * width,
    )
    message = call(
        last_message_kernel, kept((chips, own, feat + chips * 2 * rank)), place, half_mine, core_swap(half_other)
    )
    got = lax.all_to_all(message, CHIPS, 0, 0)
    grad_up = call(
        functools.partial(grad_up_kernel, factor),
        jax.ShapeDtypeStruct((2, rank, hidden), F32), place, whole, act,
        flops=4 * tokens * rank * hidden,
    )
    grad_inputs, lower_mine = call(
        last_sum_kernel,
        (jax.ShapeDtypeStruct((own, feat), BF16), kept((half, 2 * rank))), place, got, grad_one,
    )
    grad_down = call(
        functools.partial(grad_down_kernel, factor),
        jax.ShapeDtypeStruct((feat, 2 * rank), F32),
        place, mine, other, next_mine, next_other, lower_mine, core_swap(lower_mine),
        flops=4 * tokens * feat * rank,
    )
    return grad_inputs.reshape(1, micro, rows, feat), grad_down[None], grad_up[None]


def solution(mesh):
    sizes = dict(mesh.shape)
    fine = Mesh(
        mesh.devices.reshape(sizes["dp"] // 4, 2, 2, sizes["pipe"], sizes["tensor"]),
        ("x", "yl", "core", "pipe", "z"),
    )
    dp = ("x", "yl", "core")
    in_specs = (
        P("pipe", None, dp, "z"),
        P(None, dp, "z"),
        P("pipe", "z", None, dp),
        P("pipe", dp, "z"),
        P("pipe", "z", None),
        P("pipe", None, None, dp),
    )
    out_specs = (
        P("pipe", None, dp, "z"),
        P("pipe", "z", None),
        P("pipe", None, None, dp),
    )
    return jax.shard_map(local, mesh=fine, in_specs=in_specs, out_specs=out_specs, check_vma=False)
```

```python
import functools
import math

import jax
import jax.numpy as jnp
from jax import lax
from jax.experimental import pallas as pl
from jax.experimental.pallas import tpu as pltpu
from jax.sharding import Mesh, PartitionSpec as P

adapter_scale = 2.0
CHIPS = ("x", "yl")
F32 = jnp.float32
BF16 = jnp.bfloat16
VMEM_LIMIT = 16 * 2**20


def dot_nn(a, b):
    return jnp.dot(a, b, preferred_element_type=F32)


def dot_nt(a, b):
    return lax.dot_general(a, b, (((1,), (1,)), ((), ())), preferred_element_type=F32)


def dot_tn(a, b):
    return lax.dot_general(a, b, (((0,), (0,)), ((), ())), preferred_element_type=F32)


def kept(shape, dtype=BF16):
    return pltpu.VMEM(shape, dtype)


def call(kernel, outs, *args, scratch=(), flops=0, pin=True):
    size = sum(a.size * a.dtype.itemsize for a in args)
    return pl.pallas_call(
        kernel,
        out_shape=outs,
        in_specs=[pl.BlockSpec(memory_space=pltpu.VMEM)] * len(args),
        out_specs=jax.tree.map(lambda _: pl.BlockSpec(memory_space=pltpu.VMEM), outs),
        scratch_shapes=list(scratch),
        compiler_params=pltpu.CompilerParams(vmem_limit_bytes=VMEM_LIMIT),
        cost_estimate=pl.CostEstimate(flops=flops, bytes_accessed=size, transcendentals=0),
    )(*[pltpu.with_memory_space_constraint(a, pltpu.VMEM) if pin else a for a in args])


def core_swap(block):
    return lax.ppermute(block, "core", [(0, 1), (1, 0)])


def ring(block, step):
    n = lax.axis_size("z")
    return lax.ppermute(block, "z", [(i, (i + step) % n) for i in range(n)])


def swiglu_back(gate, up, hidden):
    sig = 1.0 / (1.0 + jnp.exp(-gate))
    gate_grad = hidden * up * sig * (1.0 + gate * (1.0 - sig))
    up_grad = hidden * gate * sig
    return gate_grad.astype(BF16), up_grad.astype(BF16)


def tiles(width, most=512):
    return [(lo, min(most, width - lo)) for lo in range(0, width, most)]


def forward_columns(x, g, weight, down, first, second, put):
    hidden, rank = second.shape[2], second.shape[1]
    low = dot_nn(x, first[...]).astype(BF16)
    put(2 * hidden, low)
    for k in range(2):
        for lo, size in tiles(hidden):
            at = k * hidden + lo
            pre = dot_nn(x, weight[:, at:at + size])
            pre += adapter_scale * dot_nn(low[:, k * rank:(k + 1) * rank], second[k, :, lo:lo + size])
            put(at, pre.astype(BF16))
    for lo, size in tiles(hidden):
        put(2 * hidden + 2 * rank + lo, dot_nt(g, down[lo:lo + size, :]).astype(BF16))


def first_kernel(mine, other, weight, down, first, second, up, back):
    rows, width = up.shape
    feat = first.shape[0]
    blocks = mine.shape[0] // rows
    far = lax.rem(lax.axis_index("z") + blocks, 2 * blocks)
    at = pl.multiple_of(lax.rem(far, blocks) * rows, rows)
    both = jnp.where(far < blocks, mine[pl.ds(at, rows), :], other[pl.ds(at, rows), :])

    def put(lo, value):
        size = value.shape[1]
        cut = min(max(width - lo, 0), size)
        if cut > 0:
            up[:, lo:lo + cut] = value[:, :cut]
        if cut < size:
            back[:, lo + cut - width:lo + size - width] = value[:, cut:]

    forward_columns(both[:, :feat], both[:, feat:], weight, down, first, second, put)


def forward_kernel(mine, other, weight, down, first, second, parts):
    n, rows, _ = parts.shape
    feat = first.shape[0]

    def put(lo, value):
        parts[:, :, lo:lo + value.shape[1]] = value.reshape(n, rows, value.shape[1])

    x = jnp.concatenate([mine[:, :feat], other[:, :feat]], axis=0)
    g = jnp.concatenate([mine[:, feat:], other[:, feat:]], axis=0)
    forward_columns(x, g, weight, down, first, second, put)


def ring_add_kernel(step, moving, parts, out):
    n, _, width = parts.shape
    size = moving.shape[1]
    part = lax.rem(lax.axis_index("z") + n + step, n)
    lo = 0 if step > 0 else width - size
    out[:, lo:lo + size] = (moving[...].astype(F32) + parts[part, :, lo:lo + size].astype(F32)).astype(BF16)
    if size < width:
        rest = width - size - lo
        out[:, rest:rest + width - size] = parts[part, :, rest:rest + width - size]


def middle_kernel(up_in, back_in, parts, sent):
    total = up_in[...].astype(F32) + back_in[...].astype(F32) + parts[lax.axis_index("z")].astype(F32)
    width = sent.shape[1]
    hidden = total.shape[1] - width
    gate, up = total[:, :hidden], total[:, hidden:2 * hidden]
    gate_grad, up_grad = swiglu_back(gate, up, total[:, width:])
    upper = lax.axis_index("pipe") == 1
    sent[:, :hidden] = jnp.where(upper, gate_grad, gate.astype(BF16))
    sent[:, hidden:2 * hidden] = jnp.where(upper, up_grad, up.astype(BF16))
    sent[:, 2 * hidden:] = total[:, 2 * hidden:width].astype(BF16)


def collect(pieces, whole):
    rows = pieces[0].shape[0]
    n = len(pieces) - 1
    far = n // 2
    for step, piece in enumerate(pieces):
        lo = pieces[far].shape[1] if step == far + 1 else 0
        distance = step if step <= far else step - 1
        at = pl.multiple_of(lax.rem(lax.axis_index("z") + distance, n) * rows, rows)
        whole[pl.ds(at, rows), lo:lo + piece.shape[1]] = piece[...]


def input_partials(act, weight, first, second, mine, other):
    feat = first.shape[0]
    hidden, rank = second.shape[2], second.shape[1]
    half = mine.shape[0]
    back = jnp.concatenate(
        [dot_nt(act[:, k * hidden:(k + 1) * hidden], second[k]) for k in range(2)], axis=1
    )
    mine[:, feat:] = back[:half]
    other[:, feat:] = back[half:].astype(BF16)
    scaled = (adapter_scale * back).astype(BF16)
    for lo, size in tiles(feat, 256):
        part = dot_nt(act[:, :2 * hidden], weight[lo:lo + size, :]) + dot_nt(scaled, first[lo:lo + size, :])
        mine[:, lo:lo + size] = part[:half]
        other[:, lo:lo + size] = part[half:].astype(BF16)


def backward_kernel(count, *refs):
    pieces = refs[:count]
    weight, first, second, whole, mine, other = refs[count:]
    collect(pieces, whole)
    input_partials(whole, weight, first, second, mine, other)


def lower_kernel(count, *refs):
    pieces = refs[:count]
    whole, weight, first, second, act, mine, other, hidden_grad = refs[count:]
    collect(pieces, hidden_grad)
    hidden = hidden_grad.shape[1]
    for lo, size in tiles(hidden, 128):
        gate_grad, up_grad = swiglu_back(
            whole[:, lo:lo + size].astype(F32),
            whole[:, hidden + lo:hidden + lo + size].astype(F32),
            hidden_grad[:, lo:lo + size].astype(F32),
        )
        act[:, lo:lo + size] = gate_grad
        act[:, hidden + lo:hidden + lo + size] = up_grad
    input_partials(act, weight, first, second, mine, other)


def spread_kernel(acts, grads, out):
    feat = acts.shape[1]
    for chip in range(out.shape[0]):
        out[chip, :, :feat] = acts[...]
        out[chip, :, feat:] = grads[...]


def add_cores_kernel(mine, other, out):
    out[...] = (mine[...] + other[...].astype(F32)).astype(BF16).reshape(out.shape)


def hand_kernel(got, out):
    total = jnp.sum(got[...].astype(F32), axis=0).astype(BF16)
    for section in range(out.shape[0]):
        for chip in range(out.shape[1]):
            out[section, chip] = total


def hidden_kernel(mine, other, down, *outs):
    *blocks, far_one, far_two, held = outs
    chips, own, feat = other.shape
    n, rows, _ = held.shape
    g = jnp.concatenate([mine[1, :, :, :feat], other[...]], axis=0).reshape(2 * chips * own, feat)
    held[...] = dot_nt(g, down[...]).astype(BF16).reshape(held.shape)
    for distance in range(n):
        block = held[lax.rem(lax.axis_index("z") + distance, n)]
        if distance == n // 2:
            cut = far_one.shape[1]
            far_one[...] = block[:, :cut]
            far_two[...] = block[:, cut:]
        else:
            blocks[distance if distance < n // 2 else distance - 1][...] = block


def pass_on_kernel(ahead, behind, three_up, three_back, far_up, far_back, up, back):
    cut = far_up.shape[1]
    total = ahead[...].astype(F32) + three_up[...].astype(F32)
    up[:, :cut] = (total[:, :cut] + far_up[...].astype(F32)).astype(BF16)
    up[:, cut:] = total[:, cut:].astype(BF16)
    total = behind[...].astype(F32) + three_back[...].astype(F32)
    back[:, :cut] = total[:, :cut].astype(BF16)
    back[:, cut:] = (total[:, cut:] + far_back[...].astype(F32)).astype(BF16)


def sum_z_kernel(*refs):
    *terms, out = refs
    total = terms[0][...].astype(F32)
    for term in terms[1:]:
        total += term[...].astype(F32)
    out[...] = total.astype(BF16)


def last_message_kernel(mine, other, out):
    total = (mine[...] + other[...].astype(F32)).astype(BF16)
    chips, rows, _ = out.shape
    wide = total.shape[1] - (out.shape[2] - total.shape[1]) // (chips - 1)
    rank = total.shape[1] - wide
    out[:, :, :wide] = total[:, :wide].reshape(chips, rows, wide)
    for chip in range(chips):
        block = total[chip * rows:(chip + 1) * rows, wide:]
        for target in range(chips):
            out[target, :, wide + chip * rank:wide + (chip + 1) * rank] = block


def last_sum_kernel(got, handed, grad, back):
    chips, rows, _ = got.shape
    feat, rank = grad.shape[1], back.shape[1]
    total = jnp.sum(got[...].astype(F32), axis=0).astype(BF16)
    upper = lax.axis_index("pipe") == 1
    grad[...] = jnp.where(upper, handed[1, lax.axis_index(CHIPS), :, :feat], total[:, :feat])
    for chip in range(chips):
        held = jnp.where(upper, handed[1, chip, :, feat:], total[:, feat + chip * rank:feat + (chip + 1) * rank])
        back[chip * rows:(chip + 1) * rows, :] = held


def grad_up_kernel(factor, whole, act, out):
    hidden, rank = out.shape[2], out.shape[1]
    for k in range(2):
        low = whole[:, 2 * hidden + k * rank:2 * hidden + (k + 1) * rank]
        for lo, size in tiles(hidden):
            at = k * hidden + lo
            used = jnp.where(lax.axis_index("pipe") == 1, whole[:, at:at + size], act[:, at:at + size])
            out[k, :, lo:lo + size] = dot_tn(low, used) * factor


def grad_down_kernel(inputs, back, out):
    for lo, size in tiles(out.shape[0], 256):
        out[lo:lo + size, :] = dot_tn(inputs[:, lo:lo + size], back[...])


def grad_down_end_kernel(factor, inputs, back, half, out):
    for lo, size in tiles(out.shape[0], 256):
        part = half[lo:lo + size, :] + dot_tn(inputs[:, lo:lo + size], back[...])
        out[lo:lo + size, :] = part * factor


def local(acts, output_gradient, gate_up_weight, down, adapter_first_weight, adapter_second_weight):
    micro, rows, feat = acts.shape[1:]
    hidden = down.shape[1]
    rank = adapter_second_weight.shape[2]
    own = micro * rows
    weight = gate_up_weight[0].reshape(feat, 2 * hidden)
    down_weight = down[0]
    first = adapter_first_weight[0]
    second = adapter_second_weight[0]
    chips = lax.axis_size(CHIPS)
    tokens = own * chips * lax.axis_size("core")
    half = tokens // 2
    n = lax.axis_size("z")
    block = tokens // n
    width = 2 * hidden + 2 * rank
    factor = adapter_scale / math.sqrt(tokens)

    def gather_z(piece):
        cut = piece.shape[1] // 256 * 128
        ahead_two, behind_two = ring(piece, -2), ring(piece, 2)
        ahead, behind = ring(piece, -1), ring(piece, 1)
        ahead_three, behind_three = ring(ahead_two, -1), ring(behind_two, 1)
        far = [ring(ahead_two[:, :cut], -2), ring(behind_two[:, cut:], 2)]
        return [piece, ahead, ahead_two, ahead_three] + far + [behind_three, behind_two, behind]

    message = call(
        spread_kernel, kept((chips, own, 2 * feat)),
        acts[0].reshape(own, feat), output_gradient.reshape(own, feat),
        pin=False,
    )
    mine = lax.all_to_all(message, CHIPS, 0, 0).reshape(half, 2 * feat)
    other = core_swap(mine)

    full = width + hidden
    up, back = call(
        first_kernel, (kept((block, full // 2)), kept((block, full // 2))),
        mine, other, weight, down_weight, first, second,
        flops=2 * block * feat * full,
    )
    parts = call(
        forward_kernel, kept((n, block, full)),
        mine, other, weight, down_weight, first, second,
        flops=2 * tokens * feat * full,
    )
    for step in range(n // 2 - 1, -1, -1):
        up, back = ring(up, 1), ring(back, -1)
        if step:
            up = call(functools.partial(ring_add_kernel, step), kept((block, full)), up, parts)
            back = call(functools.partial(ring_add_kernel, -step), kept((block, full)), back, parts)
    sent = call(middle_kernel, kept((block, width)), up, back, parts)
    whole, half_mine, half_other = call(
        functools.partial(backward_kernel, n + 1),
        (kept((tokens, width)), kept((half, feat + 2 * rank), F32), kept((half, feat + 2 * rank))),
        *gather_z(sent), weight, first, second,
        flops=2 * tokens * feat * width,
    )
    shape = (chips, own, feat + 2 * rank)
    message = call(add_cores_kernel, kept(shape), half_mine, core_swap(half_other))
    message = call(hand_kernel, kept((2,) + shape), lax.all_to_all(message, CHIPS, 0, 0))

    handed = lax.all_to_all(message.reshape((2 * chips,) + shape[1:]), ("pipe",) + CHIPS, 0, 0)
    handed = handed.reshape((2,) + shape)
    cut = hidden // 256 * 128
    zero, one, two, three, minus_three, minus_two, minus_one, far_one, far_two = call(
        hidden_kernel,
        (kept((block, hidden)),) * (n - 1) + (kept((block, cut)), kept((block, hidden - cut))),
        handed, core_swap(handed[1, :, :, :feat]), down_weight,
        scratch=[pltpu.VMEM((n, block, hidden), BF16)],
        flops=2 * tokens * feat * hidden,
    )
    up, back = call(
        pass_on_kernel, (kept((block, hidden)),) * 2,
        two, minus_two, ring(three, 1), ring(minus_three, -1), ring(far_one, 2), ring(far_two, -2),
    )
    message = call(
        sum_z_kernel, kept((block, hidden)),
        zero, ring(one, 1), ring(minus_one, -1), ring(up, 2), ring(back, -2),
    )
    act, half_mine, half_other = call(
        functools.partial(lower_kernel, n + 1),
        (kept((tokens, 2 * hidden)), kept((half, feat + 2 * rank), F32), kept((half, feat + 2 * rank))),
        *gather_z(message), whole, weight, first, second,
        scratch=[pltpu.VMEM((tokens, hidden), BF16)],
        flops=2 * tokens * feat * width,
    )
    grad_up = call(
        functools.partial(grad_up_kernel, factor),
        jax.ShapeDtypeStruct((2, rank, hidden), F32), whole, act,
        flops=4 * tokens * rank * hidden,
    )
    half_mine, grad_up = lax.optimization_barrier((half_mine, grad_up))
    message = call(
        last_message_kernel, kept((chips, own, feat + chips * 2 * rank)), half_mine, core_swap(half_other)
    )
    got = lax.all_to_all(message, CHIPS, 0, 0)
    grad_inputs, back_mine = call(
        last_sum_kernel,
        (jax.ShapeDtypeStruct((own, feat), BF16), kept((half, 2 * rank))), got, handed,
    )
    grad_down = call(
        grad_down_kernel, kept((feat, 2 * rank), F32), mine, back_mine,
        flops=2 * tokens * feat * rank,
    )
    grad_down = call(
        functools.partial(grad_down_end_kernel, factor),
        jax.ShapeDtypeStruct((feat, 2 * rank), F32), other, core_swap(back_mine), grad_down,
        flops=2 * tokens * feat * rank,
    )
    return grad_inputs.reshape(1, micro, rows, feat), grad_down[None], grad_up[None]


def solution(mesh):
    sizes = dict(mesh.shape)
    fine = Mesh(
        mesh.devices.reshape(sizes["dp"] // 4, 2, 2, sizes["pipe"], sizes["tensor"]),
        ("x", "yl", "core", "pipe", "z"),
    )
    dp = ("x", "yl", "core")
    in_specs = (
        P("pipe", None, dp, "z"),
        P(None, dp, "z"),
        P("pipe", "z", None, dp),
        P("pipe", dp, "z"),
        P("pipe", "z", None),
        P("pipe", None, None, dp),
    )
    out_specs = (
        P("pipe", None, dp, "z"),
        P("pipe", "z", None),
        P("pipe", None, None, dp),
    )
    return jax.shard_map(local, mesh=fine, in_specs=in_specs, out_specs=out_specs, check_vma=False)
```

```python
import functools
import math

import jax
import jax.numpy as jnp
from jax import lax
from jax.experimental import pallas as pl
from jax.experimental.pallas import tpu as pltpu
from jax.sharding import Mesh, PartitionSpec as P

adapter_scale = 2.0
CHIPS = ("x", "yl")
F32 = jnp.float32
BF16 = jnp.bfloat16
VMEM_LIMIT = 16 * 2**20


def dot_nn(a, b):
    return jnp.dot(a, b, preferred_element_type=F32)


def dot_nt(a, b):
    return lax.dot_general(a, b, (((1,), (1,)), ((), ())), preferred_element_type=F32)


def dot_tn(a, b):
    return lax.dot_general(a, b, (((0,), (0,)), ((), ())), preferred_element_type=F32)


def kept(shape, dtype=BF16):
    return pltpu.VMEM(shape, dtype)


def call(kernel, outs, *args, scratch=(), flops=0, pin=True):
    size = sum(a.size * a.dtype.itemsize for a in args)
    return pl.pallas_call(
        kernel,
        out_shape=outs,
        in_specs=[pl.BlockSpec(memory_space=pltpu.VMEM)] * len(args),
        out_specs=jax.tree.map(lambda _: pl.BlockSpec(memory_space=pltpu.VMEM), outs),
        scratch_shapes=list(scratch),
        compiler_params=pltpu.CompilerParams(vmem_limit_bytes=VMEM_LIMIT),
        cost_estimate=pl.CostEstimate(flops=flops, bytes_accessed=size, transcendentals=0),
    )(*[pltpu.with_memory_space_constraint(a, pltpu.VMEM) if pin else a for a in args])


def core_swap(block):
    return lax.ppermute(block, "core", [(0, 1), (1, 0)])


def ring(block, step):
    n = lax.axis_size("z")
    return lax.ppermute(block, "z", [(i, (i + step) % n) for i in range(n)])


def swiglu_back(gate, up, hidden):
    sig = 1.0 / (1.0 + jnp.exp(-gate))
    gate_grad = hidden * up * sig * (1.0 + gate * (1.0 - sig))
    up_grad = hidden * gate * sig
    return gate_grad.astype(BF16), up_grad.astype(BF16)


def tiles(width, most=512):
    return [(lo, min(most, width - lo)) for lo in range(0, width, most)]


def forward_columns(x, g, weight, down, first, second, put):
    hidden, rank = second.shape[2], second.shape[1]
    low = dot_nn(x, first[...]).astype(BF16)
    put(2 * hidden, low)
    for k in range(2):
        for lo, size in tiles(hidden):
            at = k * hidden + lo
            pre = dot_nn(x, weight[:, at:at + size])
            pre += adapter_scale * dot_nn(low[:, k * rank:(k + 1) * rank], second[k, :, lo:lo + size])
            put(at, pre.astype(BF16))
    for lo, size in tiles(hidden):
        put(2 * hidden + 2 * rank + lo, dot_nt(g, down[lo:lo + size, :]).astype(BF16))


def first_kernel(mine, other, weight, down, first, second, up, back):
    rows, width = up.shape
    feat = first.shape[0]
    blocks = mine.shape[0] // rows
    far = lax.rem(lax.axis_index("z") + blocks, 2 * blocks)
    at = pl.multiple_of(lax.rem(far, blocks) * rows, rows)
    both = jnp.where(far < blocks, mine[pl.ds(at, rows), :], other[pl.ds(at, rows), :])

    def put(lo, value):
        size = value.shape[1]
        cut = min(max(width - lo, 0), size)
        if cut > 0:
            up[:, lo:lo + cut] = value[:, :cut]
        if cut < size:
            back[:, lo + cut - width:lo + size - width] = value[:, cut:]

    forward_columns(both[:, :feat], both[:, feat:], weight, down, first, second, put)


def forward_kernel(mine, other, weight, down, first, second, parts):
    n, rows, _ = parts.shape
    feat = first.shape[0]

    def put(lo, value):
        parts[:, :, lo:lo + value.shape[1]] = value.reshape(n, rows, value.shape[1])

    x = jnp.concatenate([mine[:, :feat], other[:, :feat]], axis=0)
    g = jnp.concatenate([mine[:, feat:], other[:, feat:]], axis=0)
    forward_columns(x, g, weight, down, first, second, put)


def ring_add_kernel(step, moving, parts, out):
    n, _, width = parts.shape
    size = moving.shape[1]
    part = lax.rem(lax.axis_index("z") + n + step, n)
    lo = 0 if step > 0 else width - size
    out[:, lo:lo + size] = (moving[...].astype(F32) + parts[part, :, lo:lo + size].astype(F32)).astype(BF16)
    if size < width:
        rest = width - size - lo
        out[:, rest:rest + width - size] = parts[part, :, rest:rest + width - size]


def middle_kernel(up_in, back_in, parts, sent):
    total = up_in[...].astype(F32) + back_in[...].astype(F32) + parts[lax.axis_index("z")].astype(F32)
    width = sent.shape[1]
    hidden = total.shape[1] - width
    gate, up = total[:, :hidden], total[:, hidden:2 * hidden]
    gate_grad, up_grad = swiglu_back(gate, up, total[:, width:])
    upper = lax.axis_index("pipe") == 1
    sent[:, :hidden] = jnp.where(upper, gate_grad, gate.astype(BF16))
    sent[:, hidden:2 * hidden] = jnp.where(upper, up_grad, up.astype(BF16))
    sent[:, 2 * hidden:] = total[:, 2 * hidden:width].astype(BF16)


def collect(n, pieces, whole):
    rows = pieces[0].shape[0]
    split = len(pieces) - n
    for step, piece in enumerate(pieces):
        distance = step if step <= n // 2 else step - split
        lo = pieces[n // 2].shape[1] if split and step == n // 2 + 1 else 0
        at = pl.multiple_of(lax.rem(lax.axis_index("z") + distance, n) * rows, rows)
        whole[pl.ds(at, rows), lo:lo + piece.shape[1]] = piece[...]


def input_partials(act, weight, first, second, mine, other):
    feat = first.shape[0]
    hidden, rank = second.shape[2], second.shape[1]
    half = mine.shape[0]
    back = jnp.concatenate(
        [dot_nt(act[:, k * hidden:(k + 1) * hidden], second[k]) for k in range(2)], axis=1
    )
    mine[:, feat:] = back[:half]
    other[:, feat:] = back[half:].astype(BF16)
    scaled = (adapter_scale * back).astype(BF16)
    for lo, size in tiles(feat, 256):
        part = dot_nt(act[:, :2 * hidden], weight[lo:lo + size, :]) + dot_nt(scaled, first[lo:lo + size, :])
        mine[:, lo:lo + size] = part[:half]
        other[:, lo:lo + size] = part[half:].astype(BF16)


def backward_kernel(count, *refs):
    pieces = refs[:count]
    weight, first, second, whole, mine, other = refs[count:]
    collect(lax.axis_size("z"), pieces, whole)
    input_partials(whole, weight, first, second, mine, other)


def lower_kernel(count, *refs):
    pieces = refs[:count]
    whole, weight, first, second, act, mine, other, hidden_grad = refs[count:]
    collect(lax.axis_size("z"), pieces, hidden_grad)
    hidden = hidden_grad.shape[1]
    for lo, size in tiles(hidden, 128):
        gate_grad, up_grad = swiglu_back(
            whole[:, lo:lo + size].astype(F32),
            whole[:, hidden + lo:hidden + lo + size].astype(F32),
            hidden_grad[:, lo:lo + size].astype(F32),
        )
        act[:, lo:lo + size] = gate_grad
        act[:, hidden + lo:hidden + lo + size] = up_grad
    input_partials(act, weight, first, second, mine, other)


def spread_kernel(acts, grads, out):
    feat = acts.shape[1]
    for chip in range(out.shape[0]):
        out[chip, :, :feat] = acts[...]
        out[chip, :, feat:] = grads[...]


def add_cores_kernel(mine, other, out):
    out[...] = (mine[...] + other[...].astype(F32)).astype(BF16).reshape(out.shape)


def hand_kernel(got, out):
    total = jnp.sum(got[...].astype(F32), axis=0).astype(BF16)
    for section in range(out.shape[0]):
        for chip in range(out.shape[1]):
            out[section, chip] = total


def hidden_kernel(mine, other, down, *outs):
    *blocks, held = outs
    chips, own, feat = other.shape
    n, rows, _ = held.shape
    g = jnp.concatenate([mine[1, :, :, :feat], other[...]], axis=0).reshape(2 * chips * own, feat)
    held[...] = dot_nt(g, down[...]).astype(BF16).reshape(held.shape)
    for distance in range(n):
        blocks[distance][...] = held[lax.rem(lax.axis_index("z") + distance, n)]


def add_kernel(*refs):
    *terms, out = refs
    total = terms[0][...].astype(F32)
    for term in terms[1:]:
        total += term[...].astype(F32)
    out[...] = total.astype(BF16)


def last_message_kernel(mine, other, out):
    total = (mine[...] + other[...].astype(F32)).astype(BF16)
    chips, rows, _ = out.shape
    wide = total.shape[1] - (out.shape[2] - total.shape[1]) // (chips - 1)
    rank = total.shape[1] - wide
    out[:, :, :wide] = total[:, :wide].reshape(chips, rows, wide)
    for chip in range(chips):
        block = total[chip * rows:(chip + 1) * rows, wide:]
        for target in range(chips):
            out[target, :, wide + chip * rank:wide + (chip + 1) * rank] = block


def last_sum_kernel(got, handed, grad, back):
    chips, rows, _ = got.shape
    feat, rank = grad.shape[1], back.shape[1]
    total = jnp.sum(got[...].astype(F32), axis=0).astype(BF16)
    upper = lax.axis_index("pipe") == 1
    grad[...] = jnp.where(upper, handed[1, lax.axis_index(CHIPS), :, :feat], total[:, :feat])
    for chip in range(chips):
        held = jnp.where(upper, handed[1, chip, :, feat:], total[:, feat + chip * rank:feat + (chip + 1) * rank])
        back[chip * rows:(chip + 1) * rows, :] = held


def grad_up_kernel(factor, whole, act, out):
    hidden, rank = out.shape[2], out.shape[1]
    for k in range(2):
        low = whole[:, 2 * hidden + k * rank:2 * hidden + (k + 1) * rank]
        for lo, size in tiles(hidden):
            at = k * hidden + lo
            used = jnp.where(lax.axis_index("pipe") == 1, whole[:, at:at + size], act[:, at:at + size])
            out[k, :, lo:lo + size] = dot_tn(low, used) * factor


def grad_down_kernel(inputs, back, out):
    for lo, size in tiles(out.shape[0], 256):
        out[lo:lo + size, :] = dot_tn(inputs[:, lo:lo + size], back[...])


def grad_down_end_kernel(factor, inputs, back, half, out):
    for lo, size in tiles(out.shape[0], 256):
        part = half[lo:lo + size, :] + dot_tn(inputs[:, lo:lo + size], back[...])
        out[lo:lo + size, :] = part * factor


def local(acts, output_gradient, gate_up_weight, down, adapter_first_weight, adapter_second_weight):
    micro, rows, feat = acts.shape[1:]
    hidden = down.shape[1]
    rank = adapter_second_weight.shape[2]
    own = micro * rows
    weight = gate_up_weight[0].reshape(feat, 2 * hidden)
    down_weight = down[0]
    first = adapter_first_weight[0]
    second = adapter_second_weight[0]
    chips = lax.axis_size(CHIPS)
    tokens = own * chips * lax.axis_size("core")
    half = tokens // 2
    n = lax.axis_size("z")
    block = tokens // n
    width = 2 * hidden + 2 * rank
    factor = adapter_scale / math.sqrt(tokens)

    def gather_z(piece, halves):
        cut = piece.shape[1] // 256 * 128
        ahead_two, behind_two = ring(piece, -2), ring(piece, 2)
        ahead, behind = ring(piece, -1), ring(piece, 1)
        ahead_three, behind_three = ring(ahead_two, -1), ring(behind_two, 1)
        if halves:
            far = [ring(ahead_two[:, :cut], -2), ring(behind_two[:, cut:], 2)]
        else:
            far = [ring(ahead_two, -2)]
        return [piece, ahead, ahead_two, ahead_three] + far + [behind_three, behind_two, behind]

    message = call(
        spread_kernel, kept((chips, own, 2 * feat)),
        acts[0].reshape(own, feat), output_gradient.reshape(own, feat),
        pin=False,
    )
    mine = lax.all_to_all(message, CHIPS, 0, 0).reshape(half, 2 * feat)
    other = core_swap(mine)

    full = width + hidden
    up, back = call(
        first_kernel, (kept((block, full // 2)), kept((block, full // 2))),
        mine, other, weight, down_weight, first, second,
        flops=2 * block * feat * full,
    )
    parts = call(
        forward_kernel, kept((n, block, full)),
        mine, other, weight, down_weight, first, second,
        flops=2 * tokens * feat * full,
    )
    for step in range(n // 2 - 1, -1, -1):
        up, back = ring(up, 1), ring(back, -1)
        if step:
            up = call(functools.partial(ring_add_kernel, step), kept((block, full)), up, parts)
            back = call(functools.partial(ring_add_kernel, -step), kept((block, full)), back, parts)
    sent = call(middle_kernel, kept((block, width)), up, back, parts)
    whole, half_mine, half_other = call(
        functools.partial(backward_kernel, n),
        (kept((tokens, width)), kept((half, feat + 2 * rank), F32), kept((half, feat + 2 * rank))),
        *gather_z(sent, False), weight, first, second,
        flops=2 * tokens * feat * width,
    )
    shape = (chips, own, feat + 2 * rank)
    message = call(add_cores_kernel, kept(shape), half_mine, core_swap(half_other))
    message = call(hand_kernel, kept((2,) + shape), lax.all_to_all(message, CHIPS, 0, 0))

    handed = lax.all_to_all(message.reshape((2 * chips,) + shape[1:]), ("pipe",) + CHIPS, 0, 0)
    handed = handed.reshape((2,) + shape)
    zero, one, two, three, far, minus_three, minus_two, minus_one = call(
        hidden_kernel, (kept((block, hidden)),) * n,
        handed, core_swap(handed[1, :, :, :feat]), down_weight,
        scratch=[pltpu.VMEM((n, block, hidden), BF16)],
        flops=2 * tokens * feat * hidden,
    )
    up = call(add_kernel, kept((block, hidden)), two, ring(three, 1), ring(far, 2))
    back = call(add_kernel, kept((block, hidden)), minus_two, ring(minus_three, -1))
    summed = call(
        add_kernel, kept((block, hidden)), zero, ring(one, 1), ring(minus_one, -1), ring(up, 2), ring(back, -2)
    )
    act, half_mine, half_other = call(
        functools.partial(lower_kernel, n),
        (kept((tokens, 2 * hidden)), kept((half, feat + 2 * rank), F32), kept((half, feat + 2 * rank))),
        *gather_z(summed, False), whole, weight, first, second,
        scratch=[pltpu.VMEM((tokens, hidden), BF16)],
        flops=2 * tokens * feat * width,
    )
    grad_up = call(
        functools.partial(grad_up_kernel, factor),
        jax.ShapeDtypeStruct((2, rank, hidden), F32), whole, act,
        flops=4 * tokens * rank * hidden,
    )
    half_mine, grad_up = lax.optimization_barrier((half_mine, grad_up))
    message = call(
        last_message_kernel, kept((chips, own, feat + chips * 2 * rank)), half_mine, core_swap(half_other)
    )
    got = lax.all_to_all(message, CHIPS, 0, 0)
    grad_inputs, back_mine = call(
        last_sum_kernel,
        (jax.ShapeDtypeStruct((own, feat), BF16), kept((half, 2 * rank))), got, handed,
    )
    grad_down = call(
        grad_down_kernel, kept((feat, 2 * rank), F32), mine, back_mine,
        flops=2 * tokens * feat * rank,
    )
    grad_down = call(
        functools.partial(grad_down_end_kernel, factor),
        jax.ShapeDtypeStruct((feat, 2 * rank), F32), other, core_swap(back_mine), grad_down,
        flops=2 * tokens * feat * rank,
    )
    return grad_inputs.reshape(1, micro, rows, feat), grad_down[None], grad_up[None]


def solution(mesh):
    sizes = dict(mesh.shape)
    fine = Mesh(
        mesh.devices.reshape(sizes["dp"] // 4, 2, 2, sizes["pipe"], sizes["tensor"]),
        ("x", "yl", "core", "pipe", "z"),
    )
    dp = ("x", "yl", "core")
    in_specs = (
        P("pipe", None, dp, "z"),
        P(None, dp, "z"),
        P("pipe", "z", None, dp),
        P("pipe", dp, "z"),
        P("pipe", "z", None),
        P("pipe", None, None, dp),
    )
    out_specs = (
        P("pipe", None, dp, "z"),
        P("pipe", "z", None),
        P("pipe", None, None, dp),
    )
    return jax.shard_map(local, mesh=fine, in_specs=in_specs, out_specs=out_specs, check_vma=False)
```

```python
import functools
import math

import jax
import jax.numpy as jnp
from jax import lax
from jax.experimental import pallas as pl
from jax.experimental.pallas import tpu as pltpu
from jax.sharding import Mesh, PartitionSpec as P

adapter_scale = 2.0
CHIPS = ("x", "yl")
F32 = jnp.float32
BF16 = jnp.bfloat16
VMEM_LIMIT = 16 * 2**20


def dot_nn(a, b):
    return jnp.dot(a, b, preferred_element_type=F32)


def dot_nt(a, b):
    return lax.dot_general(a, b, (((1,), (1,)), ((), ())), preferred_element_type=F32)


def dot_tn(a, b):
    return lax.dot_general(a, b, (((0,), (0,)), ((), ())), preferred_element_type=F32)


def kept(shape, dtype=BF16):
    return pltpu.VMEM(shape, dtype)


def call(kernel, outs, *args, scratch=(), flops=0, pin=True):
    size = sum(a.size * a.dtype.itemsize for a in args)
    return pl.pallas_call(
        kernel,
        out_shape=outs,
        in_specs=[pl.BlockSpec(memory_space=pltpu.VMEM)] * len(args),
        out_specs=jax.tree.map(lambda _: pl.BlockSpec(memory_space=pltpu.VMEM), outs),
        scratch_shapes=list(scratch),
        compiler_params=pltpu.CompilerParams(vmem_limit_bytes=VMEM_LIMIT),
        cost_estimate=pl.CostEstimate(flops=flops, bytes_accessed=size, transcendentals=0),
    )(*[pltpu.with_memory_space_constraint(a, pltpu.VMEM) if pin else a for a in args])


def core_swap(block):
    return lax.ppermute(block, "core", [(0, 1), (1, 0)])


def ring(block, step):
    n = lax.axis_size("z")
    return lax.ppermute(block, "z", [(i, (i + step) % n) for i in range(n)])


def swiglu_back(gate, up, hidden):
    sig = 1.0 / (1.0 + jnp.exp(-gate))
    gate_grad = hidden * up * sig * (1.0 + gate * (1.0 - sig))
    up_grad = hidden * gate * sig
    return gate_grad.astype(BF16), up_grad.astype(BF16)


def tiles(width, most=512):
    return [(lo, min(most, width - lo)) for lo in range(0, width, most)]


def forward_columns(x, g, weight, down, first, second, put):
    hidden, rank = second.shape[2], second.shape[1]
    low = dot_nn(x, first[...]).astype(BF16)
    put(2 * hidden, low)
    for k in range(2):
        for lo, size in tiles(hidden):
            at = k * hidden + lo
            pre = dot_nn(x, weight[:, at:at + size])
            pre += adapter_scale * dot_nn(low[:, k * rank:(k + 1) * rank], second[k, :, lo:lo + size])
            put(at, pre.astype(BF16))
    for lo, size in tiles(hidden):
        put(2 * hidden + 2 * rank + lo, dot_nt(g, down[lo:lo + size, :]).astype(BF16))


def first_kernel(mine, other, weight, down, first, second, up, back):
    rows, width = up.shape
    feat = first.shape[0]
    blocks = mine.shape[0] // rows
    far = lax.rem(lax.axis_index("z") + blocks, 2 * blocks)
    at = pl.multiple_of(lax.rem(far, blocks) * rows, rows)
    both = jnp.where(far < blocks, mine[pl.ds(at, rows), :], other[pl.ds(at, rows), :])

    def put(lo, value):
        size = value.shape[1]
        cut = min(max(width - lo, 0), size)
        if cut > 0:
            up[:, lo:lo + cut] = value[:, :cut]
        if cut < size:
            back[:, lo + cut - width:lo + size - width] = value[:, cut:]

    forward_columns(both[:, :feat], both[:, feat:], weight, down, first, second, put)


def forward_kernel(mine, other, weight, down, first, second, parts):
    n, rows, _ = parts.shape
    feat = first.shape[0]

    def put(lo, value):
        parts[:, :, lo:lo + value.shape[1]] = value.reshape(n, rows, value.shape[1])

    x = jnp.concatenate([mine[:, :feat], other[:, :feat]], axis=0)
    g = jnp.concatenate([mine[:, feat:], other[:, feat:]], axis=0)
    forward_columns(x, g, weight, down, first, second, put)


def ring_add_kernel(step, moving, parts, out):
    n, _, width = parts.shape
    size = moving.shape[1]
    part = lax.rem(lax.axis_index("z") + n + step, n)
    lo = 0 if step > 0 else width - size
    out[:, lo:lo + size] = (moving[...].astype(F32) + parts[part, :, lo:lo + size].astype(F32)).astype(BF16)
    if size < width:
        rest = width - size - lo
        out[:, rest:rest + width - size] = parts[part, :, rest:rest + width - size]


def middle_kernel(up_in, back_in, parts, sent):
    total = up_in[...].astype(F32) + back_in[...].astype(F32) + parts[lax.axis_index("z")].astype(F32)
    width = sent.shape[1]
    hidden = total.shape[1] - width
    gate, up = total[:, :hidden], total[:, hidden:2 * hidden]
    gate_grad, up_grad = swiglu_back(gate, up, total[:, width:])
    upper = lax.axis_index("pipe") == 1
    sent[:, :hidden] = jnp.where(upper, gate_grad, gate.astype(BF16))
    sent[:, hidden:2 * hidden] = jnp.where(upper, up_grad, up.astype(BF16))
    sent[:, 2 * hidden:] = total[:, 2 * hidden:width].astype(BF16)


def collect(n, pieces, whole):
    rows = pieces[0].shape[0]
    split = len(pieces) - n
    for step, piece in enumerate(pieces):
        distance = step if step <= n // 2 else step - split
        lo = pieces[n // 2].shape[1] if split and step == n // 2 + 1 else 0
        at = pl.multiple_of(lax.rem(lax.axis_index("z") + distance, n) * rows, rows)
        whole[pl.ds(at, rows), lo:lo + piece.shape[1]] = piece[...]


def input_partials(act, weight, first, second, mine, other):
    feat = first.shape[0]
    hidden, rank = second.shape[2], second.shape[1]
    half = mine.shape[0]
    back = jnp.concatenate(
        [dot_nt(act[:, k * hidden:(k + 1) * hidden], second[k]) for k in range(2)], axis=1
    )
    mine[:, feat:] = back[:half]
    other[:, feat:] = back[half:].astype(BF16)
    scaled = (adapter_scale * back).astype(BF16)
    for lo, size in tiles(feat, 256):
        part = dot_nt(act[:, :2 * hidden], weight[lo:lo + size, :]) + dot_nt(scaled, first[lo:lo + size, :])
        mine[:, lo:lo + size] = part[:half]
        other[:, lo:lo + size] = part[half:].astype(BF16)


def backward_kernel(count, *refs):
    pieces = refs[:count]
    weight, first, second, whole, mine, other = refs[count:]
    collect(lax.axis_size("z"), pieces, whole)
    input_partials(whole, weight, first, second, mine, other)


def lower_kernel(count, *refs):
    pieces = refs[:count]
    whole, weight, first, second, act, mine, other, hidden_grad = refs[count:]
    collect(lax.axis_size("z"), pieces, hidden_grad)
    hidden = hidden_grad.shape[1]
    for lo, size in tiles(hidden, 128):
        gate_grad, up_grad = swiglu_back(
            whole[:, lo:lo + size].astype(F32),
            whole[:, hidden + lo:hidden + lo + size].astype(F32),
            hidden_grad[:, lo:lo + size].astype(F32),
        )
        act[:, lo:lo + size] = gate_grad
        act[:, hidden + lo:hidden + lo + size] = up_grad
    input_partials(act, weight, first, second, mine, other)


def spread_kernel(rows, out):
    for chip in range(out.shape[0]):
        out[chip] = rows[...]


def add_cores_kernel(mine, other, out):
    out[...] = (mine[...] + other[...].astype(F32)).astype(BF16).reshape(out.shape)


def hand_kernel(got, back, out):
    total = jnp.sum(got[...].astype(F32), axis=0).astype(BF16)
    feat = out.shape[3]
    back[...] = total[:, feat:]
    for section in range(out.shape[0]):
        for chip in range(out.shape[1]):
            out[section, chip] = total[:, :feat]


def hidden_kernel(mine, other, down, *outs):
    *blocks, held = outs
    chips, own, feat = other.shape
    n, rows, _ = held.shape
    g = jnp.concatenate([mine[1], other[...]], axis=0).reshape(2 * chips * own, feat)
    held[...] = dot_nt(g, down[...]).astype(BF16).reshape(held.shape)
    for distance in range(n):
        blocks[distance][...] = held[lax.rem(lax.axis_index("z") + distance, n)]


def add_kernel(*refs):
    *terms, out = refs
    total = terms[0][...].astype(F32)
    for term in terms[1:]:
        total += term[...].astype(F32)
    out[...] = total.astype(BF16)


def last_message_kernel(mine, other, back_one, out):
    total = (mine[...] + other[...].astype(F32)).astype(BF16)
    chips, rows, _ = out.shape
    rank = back_one.shape[1]
    wide = total.shape[1] - rank
    out[:, :, :wide] = total[:, :wide].reshape(chips, rows, wide)
    for chip in range(chips):
        block = total[chip * rows:(chip + 1) * rows, wide:]
        for target in range(chips):
            out[target, :, wide + chip * rank:wide + (chip + 1) * rank] = block

    @pl.when(lax.axis_index("pipe") == 1)
    def _():
        for target in range(chips):
            out[target, :, :rank] = back_one[...]


def last_sum_kernel(got, handed, grad, back):
    chips, rows, _ = got.shape
    feat, rank = grad.shape[1], back.shape[1]
    total = jnp.sum(got[...].astype(F32), axis=0).astype(BF16)
    upper = lax.axis_index("pipe") == 1
    grad[...] = jnp.where(upper, handed[1, lax.axis_index(CHIPS)], total[:, :feat])
    for chip in range(chips):
        held = jnp.where(upper, got[chip, :, :rank], total[:, feat + chip * rank:feat + (chip + 1) * rank])
        back[chip * rows:(chip + 1) * rows, :] = held


def grad_up_kernel(factor, whole, act, out):
    hidden, rank = out.shape[2], out.shape[1]
    for k in range(2):
        low = whole[:, 2 * hidden + k * rank:2 * hidden + (k + 1) * rank]
        for lo, size in tiles(hidden):
            at = k * hidden + lo
            used = jnp.where(lax.axis_index("pipe") == 1, whole[:, at:at + size], act[:, at:at + size])
            out[k, :, lo:lo + size] = dot_tn(low, used) * factor


def grad_down_kernel(inputs, back, out):
    for lo, size in tiles(out.shape[0], 256):
        out[lo:lo + size, :] = dot_tn(inputs[:, lo:lo + size], back[...])


def grad_down_end_kernel(factor, inputs, back, half, out):
    for lo, size in tiles(out.shape[0], 256):
        part = half[lo:lo + size, :] + dot_tn(inputs[:, lo:lo + size], back[...])
        out[lo:lo + size, :] = part * factor


def local(acts, output_gradient, gate_up_weight, down, adapter_first_weight, adapter_second_weight):
    micro, rows, feat = acts.shape[1:]
    hidden = down.shape[1]
    rank = adapter_second_weight.shape[2]
    own = micro * rows
    weight = gate_up_weight[0].reshape(feat, 2 * hidden)
    down_weight = down[0]
    first = adapter_first_weight[0]
    second = adapter_second_weight[0]
    chips = lax.axis_size(CHIPS)
    tokens = own * chips * lax.axis_size("core")
    half = tokens // 2
    n = lax.axis_size("z")
    block = tokens // n
    width = 2 * hidden + 2 * rank
    factor = adapter_scale / math.sqrt(tokens)

    def gather_z(piece, halves):
        cut = piece.shape[1] // 256 * 128
        ahead_two, behind_two = ring(piece, -2), ring(piece, 2)
        ahead, behind = ring(piece, -1), ring(piece, 1)
        ahead_three, behind_three = ring(ahead_two, -1), ring(behind_two, 1)
        if halves:
            far = [ring(ahead_two[:, :cut], -2), ring(behind_two[:, cut:], 2)]
        else:
            far = [ring(ahead_two, -2)]
        return [piece, ahead, ahead_two, ahead_three] + far + [behind_three, behind_two, behind]

    message = jnp.concatenate([acts[0].reshape(own, feat), output_gradient.reshape(own, feat)], axis=1)
    message = call(spread_kernel, kept((chips, own, 2 * feat)), message)
    mine = lax.all_to_all(message, CHIPS, 0, 0).reshape(half, 2 * feat)
    other = core_swap(mine)

    full = width + hidden
    up, back = call(
        first_kernel, (kept((block, full // 2)), kept((block, full // 2))),
        mine, other, weight, down_weight, first, second,
        flops=2 * block * feat * full,
    )
    parts = call(
        forward_kernel, kept((n, block, full)),
        mine, other, weight, down_weight, first, second,
        flops=2 * tokens * feat * full,
    )
    for step in range(n // 2 - 1, -1, -1):
        up, back = ring(up, 1), ring(back, -1)
        if step:
            up = call(functools.partial(ring_add_kernel, step), kept((block, full)), up, parts)
            back = call(functools.partial(ring_add_kernel, -step), kept((block, full)), back, parts)
    sent = call(middle_kernel, kept((block, width)), up, back, parts)
    whole, half_mine, half_other = call(
        functools.partial(backward_kernel, n),
        (kept((tokens, width)), kept((half, feat + 2 * rank), F32), kept((half, feat + 2 * rank))),
        *gather_z(sent, False), weight, first, second,
        flops=2 * tokens * feat * width,
    )
    shape = (chips, own, feat)
    message = call(add_cores_kernel, kept((chips, own, feat + 2 * rank)), half_mine, core_swap(half_other))
    back_one, message = call(
        hand_kernel, (kept((own, 2 * rank)), kept((2,) + shape)), lax.all_to_all(message, CHIPS, 0, 0)
    )

    handed = lax.all_to_all(message.reshape((2 * chips,) + shape[1:]), ("pipe",) + CHIPS, 0, 0)
    handed = handed.reshape((2,) + shape)
    zero, one, two, three, far, minus_three, minus_two, minus_one = call(
        hidden_kernel, (kept((block, hidden)),) * n,
        handed, core_swap(handed[1]), down_weight,
        scratch=[pltpu.VMEM((n, block, hidden), BF16)],
        flops=2 * tokens * feat * hidden,
    )
    up = call(add_kernel, kept((block, hidden)), two, ring(three, 1), ring(far, 2))
    back = call(add_kernel, kept((block, hidden)), minus_two, ring(minus_three, -1))
    summed = call(
        add_kernel, kept((block, hidden)), zero, ring(one, 1), ring(minus_one, -1), ring(up, 2), ring(back, -2)
    )
    act, half_mine, half_other = call(
        functools.partial(lower_kernel, n),
        (kept((tokens, 2 * hidden)), kept((half, feat + 2 * rank), F32), kept((half, feat + 2 * rank))),
        *gather_z(summed, False), whole, weight, first, second,
        scratch=[pltpu.VMEM((tokens, hidden), BF16)],
        flops=2 * tokens * feat * width,
    )
    grad_up = call(
        functools.partial(grad_up_kernel, factor),
        jax.ShapeDtypeStruct((2, rank, hidden), F32), whole, act,
        flops=4 * tokens * rank * hidden,
    )
    half_mine, grad_up = lax.optimization_barrier((half_mine, grad_up))
    message = call(
        last_message_kernel, kept((chips, own, feat + chips * 2 * rank)), half_mine, core_swap(half_other),
        back_one,
    )
    got = lax.all_to_all(message, CHIPS, 0, 0)
    grad_inputs, back_mine = call(
        last_sum_kernel,
        (jax.ShapeDtypeStruct((own, feat), BF16), kept((half, 2 * rank))), got, handed,
    )
    grad_down = call(
        grad_down_kernel, kept((feat, 2 * rank), F32), mine, back_mine,
        flops=2 * tokens * feat * rank,
    )
    grad_down = call(
        functools.partial(grad_down_end_kernel, factor),
        jax.ShapeDtypeStruct((feat, 2 * rank), F32), other, core_swap(back_mine), grad_down,
        flops=2 * tokens * feat * rank,
    )
    return grad_inputs.reshape(1, micro, rows, feat), grad_down[None], grad_up[None]


def solution(mesh):
    sizes = dict(mesh.shape)
    fine = Mesh(
        mesh.devices.reshape(sizes["dp"] // 4, 2, 2, sizes["pipe"], sizes["tensor"]),
        ("x", "yl", "core", "pipe", "z"),
    )
    dp = ("x", "yl", "core")
    in_specs = (
        P("pipe", None, dp, "z"),
        P(None, dp, "z"),
        P("pipe", "z", None, dp),
        P("pipe", dp, "z"),
        P("pipe", "z", None),
        P("pipe", None, None, dp),
    )
    out_specs = (
        P("pipe", None, dp, "z"),
        P("pipe", "z", None),
        P("pipe", None, None, dp),
    )
    return jax.shard_map(local, mesh=fine, in_specs=in_specs, out_specs=out_specs, check_vma=False)
```
